512 devices in a mesh: gx: 8 (over z_lo), gy: 8 (over x, core), gz: 8 (over z_hi, y).
Axes of the slice: x: 4, y: 4, z: 16 (z_hi: 2, z_lo: 8; z = z_hi * 8 + z_lo), core: 2. Of those that a mesh axis runs over, the one named last changes fastest.
Arguments:
- tokens: bfloat16 [256, 8192], P(('gx', 'gy'), 'gz'), may hold values from -6 to 6
- gate_weight: bfloat16 [8192, 22528], P('gz', ('gx', 'gy')), may hold values from -0.0625 to 0.0625
- up_weight: bfloat16 [8192, 22528], P('gz', ('gx', 'gy')), may hold values from -0.0625 to 0.0625
- down_weight: bfloat16 [22528, 8192], P(('gx', 'gy'), 'gz'), may hold values from -0.0390625 to 0.0390625
- out_grad: bfloat16 [256, 8192], P(('gx', 'gy'), 'gz'), may hold values from -1.5 to 1.5
Outputs:
- mixed: bfloat16 [256, 8192], P(('gx', 'gy'), 'gz')
- tokens_grad: bfloat16 [256, 8192], P(('gx', 'gy'), 'gz')
- gate_grad: bfloat16 [8192, 22528], P('gz', ('gx', 'gy'))
- up_grad: bfloat16 [8192, 22528], P('gz', ('gx', 'gy'))
- down_grad: bfloat16 [22528, 8192], P(('gx', 'gy'), 'gz')
The draws below stay inside these ranges and needn't reach their ends.
All inputs are finite; a program needn't handle non-finite values.
Results may differ from the reference program's by a relative error of at most 0.0049.
Values may be sent and summed in bfloat16 or wider, within the bound.
No kernel may reach another device: no remote copies, remote signals or barrier semaphores. Data moves between devices by JAX's collectives and lax.ppermute only.
A program may use at most 64 MiB of HBM per device.

```python
import jax
import jax.numpy as jnp

D = 8192
FF = 22528
TOKENS = 256


def block_scale(key, extent, cuts, smallest, largest):
    gain, own = 1.0, jax.random.fold_in(key, 6)
    for dim, blocks in cuts:
        steps = jnp.exp(jax.random.uniform(jax.random.fold_in(own, dim), (blocks,), jnp.float32, smallest / len(cuts), largest / len(cuts)))
        gain = gain * jnp.repeat(steps, extent[dim] // blocks).reshape([-1 if axis == dim else 1 for axis in range(len(extent))])
    return gain


def normal_values(key, shape, scale, bound, pieces=(), kind=jnp.bfloat16):
    entries = scale * jax.random.normal(key, shape, jnp.float32)
    if pieces:
        entries = entries * block_scale(key, shape, pieces, -0.22, 0.18)
    return jnp.clip(entries, -bound, bound).astype(kind)


def setup_inputs(seed: int = 0) -> dict:
    splits = jax.random.split(jax.random.key(seed), 6)
    tokens = normal_values(splits[0], (TOKENS, D), 1.0, 6.0, ((0, 64), (1, 8)))
    gate_weight = normal_values(splits[1], (D, FF), D ** -0.5, 0.0625, ((0, 8), (1, 64)))
    up_weight = normal_values(splits[2], (D, FF), D ** -0.5, 0.0625, ((0, 8), (1, 64)))
    down_weight = normal_values(splits[3], (FF, D), FF ** -0.5, 0.0390625, ((0, 64), (1, 8)))
    out_grad = normal_values(splits[4], (TOKENS, D), 0.25, 1.5, ((0, 64), (1, 8)))
    return {"tokens": tokens, "gate_weight": gate_weight, "up_weight": up_weight, "down_weight": down_weight, "out_grad": out_grad}


def reference(tokens, gate_weight, up_weight, down_weight, out_grad):
    gate_val = jnp.dot(tokens, gate_weight, preferred_element_type=jnp.float32)
    up_val = jnp.dot(tokens, up_weight, preferred_element_type=jnp.float32)
    sig_val = jax.nn.sigmoid(gate_val)
    hidden = (gate_val * sig_val * up_val).astype(jnp.bfloat16)
    mixed = jnp.dot(hidden, down_weight, preferred_element_type=jnp.float32).astype(jnp.bfloat16)
    down_grad = jnp.dot(hidden.T, out_grad, preferred_element_type=jnp.float32).astype(jnp.bfloat16)
    hidden_grad = jnp.dot(out_grad, down_weight.T, preferred_element_type=jnp.float32)
    up_diff = (hidden_grad * gate_val * sig_val).astype(jnp.bfloat16)
    gate_diff = (hidden_grad * up_val * sig_val * (1.0 + gate_val * (1.0 - sig_val))).astype(jnp.bfloat16)
    gate_grad = jnp.dot(tokens.T, gate_diff, preferred_element_type=jnp.float32).astype(jnp.bfloat16)
    up_grad = jnp.dot(tokens.T, up_diff, preferred_element_type=jnp.float32).astype(jnp.bfloat16)
    tokens_grad = jnp.dot(gate_diff, gate_weight.T, preferred_element_type=jnp.float32)
    tokens_grad = tokens_grad + jnp.dot(up_diff, up_weight.T, preferred_element_type=jnp.float32)
    return mixed, tokens_grad.astype(jnp.bfloat16), gate_grad, up_grad, down_grad
```

```python
import jax
import jax.numpy as jnp
from jax import lax
from jax.sharding import Mesh, PartitionSpec as P

BF16 = jnp.bfloat16
F32 = jnp.float32


def dot(a, b, ca, cb):
    return lax.dot_general(a, b, (((ca,), (cb,)), ((), ())), preferred_element_type=F32)


def gather(part, axis):
    count = lax.axis_size(axis)
    return lax.all_to_all(jnp.broadcast_to(part[None], (count,) + part.shape), axis, 0, 0)


def swap(part, axis):
    return lax.ppermute(part, axis, [(0, 1), (1, 0)])


def on_device(tokens, gate_weight, up_weight, down_weight, out_grad):
    rows, width = tokens.shape
    n_gx, n_x, n_y = lax.axis_size("gx"), lax.axis_size("x"), lax.axis_size("y")
    units = gate_weight.shape[1]

    both = jnp.concatenate([tokens, out_grad], axis=0)
    both = gather(both, "gx").reshape(n_gx, 2, rows, width).transpose(1, 0, 2, 3)
    both = both.reshape(2, n_gx * rows, width)
    both = gather(both, "x").transpose(1, 0, 2, 3).reshape(2, n_x * n_gx * rows, width)
    other = swap(both, "core")
    tok_rows = jnp.concatenate([both[0], other[0]], axis=0)
    grad_rows = jnp.concatenate([both[1], other[1]], axis=0)
    total = tok_rows.shape[0]

    parts = jnp.stack(
        [
            dot(tok_rows, gate_weight, 1, 0).astype(BF16),
            dot(tok_rows, up_weight, 1, 0).astype(BF16),
            dot(grad_rows, down_weight, 1, 1).astype(BF16),
        ]
    )
    parts = parts.reshape(3, n_y, total // n_y, units).transpose(1, 0, 2, 3)
    share = lax.all_to_all(parts, "y", 0, 0).astype(F32).sum(axis=0)
    share = share + swap(share.astype(BF16), "zh").astype(F32)
    gate_val, up_val, hidden_grad = share[0], share[1], share[2]

    sig_val = jax.nn.sigmoid(gate_val)
    hidden = gate_val * sig_val * up_val
    up_diff = hidden_grad * gate_val * sig_val
    gate_diff = hidden_grad * up_val * sig_val * (1.0 + gate_val * (1.0 - sig_val))
    mid = jnp.stack([hidden, gate_diff, up_diff]).astype(BF16)
    mid = gather(mid, "y").transpose(1, 0, 2, 3).reshape(3, total, units)
    hidden, gate_diff, up_diff = mid[0], mid[1], mid[2]

    outs = jnp.stack(
        [
            dot(hidden, down_weight, 1, 0),
            dot(gate_diff, gate_weight, 1, 1) + dot(up_diff, up_weight, 1, 1),
        ]
    )
    half = total // 2
    outs = outs[:, :half] + swap(outs[:, half:], "core")
    outs = outs.astype(BF16).reshape(2, n_x, half // n_x, width).transpose(1, 0, 2, 3)
    outs = lax.all_to_all(outs, "x", 0, 0).astype(F32).sum(axis=0)
    outs = outs.reshape(2, n_gx, rows, width).transpose(1, 0, 2, 3)
    outs = lax.all_to_all(outs, "gx", 0, 0).sum(axis=0).astype(BF16)

    down_grad = dot(hidden, grad_rows, 0, 0).astype(BF16)
    gate_grad = dot(tok_rows, gate_diff, 0, 0).astype(BF16)
    up_grad = dot(tok_rows, up_diff, 0, 0).astype(BF16)
    return (outs[0], outs[1], gate_grad, up_grad, down_grad)


def solution(mesh):
    fine = Mesh(mesh.devices.reshape(8, 4, 2, 2, 4), ("gx", "x", "core", "zh", "y"))
    hid, dim = ("gx", "x", "core"), ("zh", "y")
    act = P(hid, dim)
    return jax.shard_map(
        on_device,
        mesh=fine,
        in_specs=(act, P(dim, hid), P(dim, hid), act, act),
        out_specs=(act, act, P(dim, hid), P(dim, hid), act),
        check_vma=False,
    )
```

```python
import math

import jax
import jax.numpy as jnp
from jax import lax
from jax.sharding import Mesh, PartitionSpec as P

BF16 = jnp.bfloat16
F16 = jnp.float16
F32 = jnp.float32
LANES = 128


def dot(a, b, ca, cb):
    return lax.dot_general(a, b, (((ca,), (cb,)), ((), ())), preferred_element_type=F32)


def gather(part, axis):
    count = lax.axis_size(axis)
    return lax.all_to_all(jnp.broadcast_to(part[None], (count,) + part.shape), axis, 0, 0)


def swap(part, axis):
    return lax.ppermute(part, axis, [(0, 1), (1, 0)])


def scales(over):
    gate = 2.0 ** math.floor(math.log2(65504 / (over * 6 * 0.0625)))
    grad = 2.0 ** math.floor(math.log2(65504 / (over * 1.5 * 0.0390625)))
    return jnp.array([gate, gate, grad], F32)[:, None, None]


def on_device(tokens, gate_weight, up_weight, down_weight, out_grad):
    rows, width = tokens.shape
    n_gx, n_x, n_y = lax.axis_size("gx"), lax.axis_size("x"), lax.axis_size("y")
    units = gate_weight.shape[1]
    wide = -(-units // LANES) * LANES

    both = jnp.concatenate([tokens, out_grad], axis=0)
    both = gather(both, "gx").reshape(n_gx, 2, rows, width).transpose(1, 0, 2, 3)
    both = both.reshape(2, n_gx * rows, width)
    both = gather(both, "x").transpose(1, 0, 2, 3).reshape(2, n_x * n_gx * rows, width)
    other = swap(both, "core")
    tok_rows = jnp.concatenate([both[0], other[0]], axis=0)
    grad_rows = jnp.concatenate([both[1], other[1]], axis=0)
    total = tok_rows.shape[0]

    first, second = scales(width), scales(width * n_y)
    parts = jnp.stack([dot(tok_rows, gate_weight, 1, 0), dot(tok_rows, up_weight, 1, 0), dot(grad_rows, down_weight, 1, 1)])
    parts = jnp.pad((parts * first).astype(F16), ((0, 0), (0, 0), (0, wide - units)))
    parts = parts.reshape(3, n_y, total // n_y, wide).transpose(1, 0, 2, 3).reshape(n_y, -1, wide)
    share = lax.all_to_all(parts, "y", 0, 0).reshape(n_y, 3, -1, wide).astype(F32).sum(axis=0) / first
    away = swap((share * second).astype(F16).reshape(-1, wide), "zh").reshape(3, -1, wide)
    share = share + away.astype(F32) / second
    gate_val, up_val, hidden_grad = share[0], share[1], share[2]

    sig_val = jax.nn.sigmoid(gate_val)
    hidden = gate_val * sig_val * up_val
    up_diff = hidden_grad * gate_val * sig_val
    gate_diff = hidden_grad * up_val * sig_val * (1.0 + gate_val * (1.0 - sig_val))
    mid = jnp.stack([hidden, gate_diff, up_diff]).astype(BF16).reshape(-1, wide)
    mid = gather(mid, "y").reshape(n_y, 3, -1, wide).transpose(1, 0, 2, 3).reshape(3, total, wide)[:, :, :units]
    hidden, gate_diff, up_diff = mid[0], mid[1], mid[2]

    outs = jnp.stack(
        [
            dot(hidden, down_weight, 1, 0),
            dot(gate_diff, gate_weight, 1, 1) + dot(up_diff, up_weight, 1, 1),
        ]
    )
    half = total // 2
    outs = outs[:, :half] + swap(outs[:, half:].astype(BF16), "core").astype(F32)
    outs = outs.astype(BF16).reshape(2, n_x, half // n_x, width).transpose(1, 0, 2, 3)
    outs = lax.all_to_all(outs, "x", 0, 0).astype(F32).sum(axis=0)
    outs = outs.astype(BF16).reshape(2, n_gx, rows, width).transpose(1, 0, 2, 3)
    outs = outs.reshape(n_gx, 2 * rows, width)
    outs = lax.all_to_all(outs, "gx", 0, 0).astype(F32).sum(axis=0).astype(BF16)

    down_grad = dot(hidden, grad_rows, 0, 0).astype(BF16)
    gate_grad = dot(tok_rows, gate_diff, 0, 0).astype(BF16)
    up_grad = dot(tok_rows, up_diff, 0, 0).astype(BF16)
    return (outs[:rows], outs[rows:], gate_grad, up_grad, down_grad)


def solution(mesh):
    fine = Mesh(mesh.devices.reshape(8, 4, 2, 2, 4), ("gx", "x", "core", "zh", "y"))
    hid, dim = ("gx", "x", "core"), ("zh", "y")
    act = P(hid, dim)
    return jax.shard_map(
        on_device,
        mesh=fine,
        in_specs=(act, P(dim, hid), P(dim, hid), act, act),
        out_specs=(act, act, P(dim, hid), P(dim, hid), act),
        check_vma=False,
    )
```

```python
import functools
import math

import jax
import jax.numpy as jnp
from jax import lax
from jax.experimental import pallas as pl
from jax.experimental.pallas import tpu as pltpu
from jax.sharding import Mesh, PartitionSpec as P

BF16 = jnp.bfloat16
F16 = jnp.float16
F32 = jnp.float32
LANES = 128
VMEM = pl.BlockSpec(memory_space=pltpu.VMEM)
LIMIT = pltpu.CompilerParams(vmem_limit_bytes=40 * 1024 * 1024)


def dot(a, b, ca, cb):
    return lax.dot_general(a, b, (((ca,), (cb,)), ((), ())), preferred_element_type=F32)


def gather(part, axis):
    count = lax.axis_size(axis)
    return lax.all_to_all(jnp.broadcast_to(part[None], (count,) + part.shape), axis, 0, 0)


def swap(part, axis):
    return lax.ppermute(part, axis, [(0, 1), (1, 0)])


def scales(over):
    gate = 2.0 ** math.floor(math.log2(65504 / (over * 6 * 0.0625)))
    grad = 2.0 ** math.floor(math.log2(65504 / (over * 1.5 * 0.0390625)))
    return gate, gate, grad


def partial_sums(scale, chunks, rows_ref, gate_ref, up_ref, down_ref, out_ref):
    n_x, _, piece, width = rows_ref.shape
    units = gate_ref.shape[0]
    share = n_x * piece // chunks
    tok = rows_ref[:, 0].reshape(n_x * piece, width)
    grad = rows_ref[:, 1].reshape(n_x * piece, width)
    parts = (dot(tok, gate_ref[...], 1, 1), dot(tok, up_ref[...], 1, 1), dot(grad, down_ref[...], 1, 1))
    for which, part in enumerate(parts):
        part = (part * scale[which]).astype(out_ref.dtype)
        for chunk in range(chunks):
            rows = pl.ds(which * share, share)
            out_ref[chunk, rows, :units] = part[chunk * share : (chunk + 1) * share]
            out_ref[chunk, rows, units:] = jnp.zeros((share, out_ref.shape[2] - units), out_ref.dtype)


def partial_outs(n_x, mid_ref, gate_ref, up_ref, down_ref, out_ref):
    chunks, _, share, wide = mid_ref.shape
    units, width = down_ref.shape
    hidden, gate_diff, up_diff = [mid_ref[:, i].reshape(chunks * share, wide)[:, :units] for i in range(3)]
    mixed = dot(hidden, down_ref[...], 1, 0)
    back = dot(gate_diff, gate_ref[...], 1, 0) + dot(up_diff, up_ref[...], 1, 0)
    out_ref[:, 0] = mixed.astype(out_ref.dtype).reshape(n_x, -1, width)
    out_ref[:, 1] = back.astype(out_ref.dtype).reshape(n_x, -1, width)


def call(body, inputs, shape, dtype):
    return pl.pallas_call(
        body,
        out_shape=jax.ShapeDtypeStruct(shape, dtype),
        in_specs=[VMEM] * len(inputs),
        out_specs=VMEM,
        compiler_params=LIMIT,
    )(*inputs)


def on_device(tokens, gate_weight, up_weight, down_weight, out_grad):
    rows, width = tokens.shape
    n_gx, n_x, n_y = lax.axis_size("gx"), lax.axis_size("x"), lax.axis_size("y")
    units = gate_weight.shape[1]
    wide = -(-units // LANES) * LANES
    weights = (gate_weight.T, up_weight.T, down_weight)
    share = 2 * n_x * n_gx * rows // n_y
    near = n_y // 2

    both = jnp.concatenate([tokens, out_grad], axis=0)
    both = gather(both, "gx").reshape(n_gx, 2, rows, width).transpose(1, 0, 2, 3)
    own = gather(both.reshape(2, n_gx * rows, width), "x")
    other = swap(own, "core")

    first, second = scales(width), scales(width * n_y)
    sums = functools.partial(partial_sums, first, near)
    shape = (near, 3 * share, wide)
    parts = jnp.concatenate(
        [call(sums, (own,) + weights, shape, F32), call(sums, (other,) + weights, shape, F32)], axis=0
    )
    parts = lax.all_to_all(parts.astype(F16), "y", 0, 0).reshape(n_y, 3, share, wide).astype(F32).sum(axis=0)
    part = [parts[i] * (1.0 / first[i]) for i in range(3)]
    away = swap(jnp.concatenate([(part[i] * second[i]).astype(F16) for i in range(3)], axis=0), "zh")
    away = away.reshape(3, share, wide).astype(F32)
    gate_val, up_val, hidden_grad = [part[i] + away[i] * (1.0 / second[i]) for i in range(3)]

    sig_val = jax.nn.sigmoid(gate_val)
    hidden = gate_val * sig_val * up_val
    up_diff = hidden_grad * gate_val * sig_val
    gate_diff = hidden_grad * up_val * sig_val * (1.0 + gate_val * (1.0 - sig_val))
    mid = jnp.concatenate([hidden.astype(BF16), gate_diff.astype(BF16), up_diff.astype(BF16)], axis=0)
    mid = gather(mid, "y").reshape(n_y, 3, share, wide)

    body = functools.partial(partial_outs, n_x)
    away = swap(call(body, (mid[near:],) + weights, own.shape, BF16), "core")
    outs = call(body, (mid[:near],) + weights, own.shape, F32)
    outs = (outs + away.astype(F32)).astype(BF16)
    outs = lax.all_to_all(outs, "x", 0, 0).astype(F32).sum(axis=0)
    outs = outs.astype(BF16).reshape(2, n_gx, rows, width).transpose(1, 0, 2, 3)
    outs = outs.reshape(n_gx, 2 * rows, width)
    outs, mid, own, other = lax.optimization_barrier((outs, mid, own, other))
    outs = lax.all_to_all(outs, "gx", 0, 0).astype(F32).sum(axis=0).astype(BF16)

    total = n_y * share
    hidden, gate_diff, up_diff = [mid[:, i].reshape(total, wide)[:, :units] for i in range(3)]
    tok_rows, grad_rows = [
        jnp.concatenate([own[:, i].reshape(total // 2, width), other[:, i].reshape(total // 2, width)], axis=0)
        for i in range(2)
    ]
    down_grad = dot(hidden, grad_rows, 0, 0).astype(BF16)
    gate_grad = dot(gate_diff, tok_rows, 0, 0).astype(BF16)
    up_grad = dot(up_diff, tok_rows, 0, 0).astype(BF16)
    return (outs[:rows], outs[rows:], gate_grad.T, up_grad.T, down_grad)


def solution(mesh):
    fine = Mesh(mesh.devices.reshape(8, 4, 2, 2, 4), ("gx", "x", "core", "zh", "y"))
    hid, dim = ("gx", "x", "core"), ("zh", "y")
    act = P(hid, dim)
    return jax.shard_map(
        on_device,
        mesh=fine,
        in_specs=(act, P(dim, hid), P(dim, hid), act, act),
        out_specs=(act, act, P(dim, hid), P(dim, hid), act),
        check_vma=False,
    )
```

```python
import functools
import math

import jax
import jax.numpy as jnp
from jax import lax
from jax.experimental import pallas as pl
from jax.experimental.pallas import tpu as pltpu
from jax.sharding import Mesh, PartitionSpec as P

BF16 = jnp.bfloat16
F16 = jnp.float16
F32 = jnp.float32
LANES = 128
VMEM = pl.BlockSpec(memory_space=pltpu.VMEM)
LIMIT = pltpu.CompilerParams(vmem_limit_bytes=40 * 1024 * 1024)


def dot(a, b, ca, cb):
    return lax.dot_general(a, b, (((ca,), (cb,)), ((), ())), preferred_element_type=F32)


def gather(part, axis):
    count = lax.axis_size(axis)
    return lax.all_to_all(jnp.broadcast_to(part[None], (count,) + part.shape), axis, 0, 0)


def swap(part, axis):
    return lax.ppermute(part, axis, [(0, 1), (1, 0)])


def scales(over):
    gate = 2.0 ** math.floor(math.log2(65504 / (over * 6 * 0.0625)))
    grad = 2.0 ** math.floor(math.log2(65504 / (over * 1.5 * 0.0390625)))
    return gate, gate, grad


def pack(block):
    rows, units = block.shape
    full = units // LANES
    rest = units - full * LANES
    if not rest:
        return jnp.concatenate([block[:, i * LANES : (i + 1) * LANES] for i in range(full)], axis=0)
    gap = LANES - rest
    kept = rows * rest // LANES
    tail = block[:, full * LANES :]
    moved = jnp.concatenate([tail[kept:, i * gap : (i + 1) * gap] for i in range(rest // gap)], axis=0)
    last = jnp.concatenate([tail[:kept], moved], axis=1)
    return jnp.concatenate([block[:, i * LANES : (i + 1) * LANES] for i in range(full)] + [last], axis=0)


def unpack(block, rows, units):
    full = units // LANES
    rest = units - full * LANES
    parts = [block[i * rows : (i + 1) * rows] for i in range(full)]
    if rest:
        gap = LANES - rest
        kept = rows * rest // LANES
        last = block[full * rows :]
        moved = last[:, rest:]
        step = rows - kept
        back = jnp.concatenate([moved[i * step : (i + 1) * step] for i in range(rest // gap)], axis=1)
        parts.append(jnp.concatenate([last[:, :rest], back], axis=0))
    return jnp.concatenate(parts, axis=1)


def partial_sums(scale, chunks, rows_ref, gate_ref, up_ref, down_ref, out_ref):
    n_x, _, piece, width = rows_ref.shape
    share = n_x * piece // chunks
    tok = rows_ref[:, 0].reshape(n_x * piece, width)
    grad = rows_ref[:, 1].reshape(n_x * piece, width)
    parts = (dot(tok, gate_ref[...], 1, 1), dot(tok, up_ref[...], 1, 1), dot(grad, down_ref[...], 1, 1))
    for which, part in enumerate(parts):
        for chunk in range(chunks):
            out_ref[chunk, which] = pack(part[chunk * share : (chunk + 1) * share] * scale[which])


def partial_outs(n_x, mid_ref, gate_ref, up_ref, down_ref, out_ref, flat_ref):
    chunks = mid_ref.shape[0]
    _, total, units = flat_ref.shape
    width = down_ref.shape[1]
    share = total // chunks
    hidden, gate_diff, up_diff = [
        jnp.concatenate([unpack(mid_ref[chunk, which], share, units) for chunk in range(chunks)], axis=0)
        for which in range(3)
    ]
    mixed = dot(hidden, down_ref[...], 1, 0)
    back = dot(gate_diff, gate_ref[...], 1, 0) + dot(up_diff, up_ref[...], 1, 0)
    out_ref[:, 0] = mixed.astype(out_ref.dtype).reshape(n_x, -1, width)
    out_ref[:, 1] = back.astype(out_ref.dtype).reshape(n_x, -1, width)
    for which, rows in enumerate((hidden, gate_diff, up_diff)):
        flat_ref[which] = rows


def call(body, inputs, *outs):
    return pl.pallas_call(
        body,
        out_shape=[jax.ShapeDtypeStruct(shape, dtype) for shape, dtype in outs],
        in_specs=[VMEM] * len(inputs),
        out_specs=[VMEM] * len(outs),
        compiler_params=LIMIT,
    )(*inputs)


def on_device(tokens, gate_weight, up_weight, down_weight, out_grad):
    rows, width = tokens.shape
    n_gx, n_x, n_y = lax.axis_size("gx"), lax.axis_size("x"), lax.axis_size("y")
    units = gate_weight.shape[1]
    weights = (gate_weight.T, up_weight.T, down_weight)
    share = 2 * n_x * n_gx * rows // n_y
    near = n_y // 2

    both = jnp.concatenate([tokens, out_grad], axis=0)
    both = gather(both, "gx").reshape(n_gx, 2, rows, width).transpose(1, 0, 2, 3)
    own = gather(both.reshape(2, n_gx * rows, width), "x")
    other = swap(own, "core")

    first, second = scales(width), scales(width * n_y)
    sums = functools.partial(partial_sums, first, near)
    shape = (near, 3, share * units // LANES, LANES)
    parts = call(sums, (own,) + weights, (shape, F32)) + call(sums, (other,) + weights, (shape, F32))
    parts = jnp.concatenate(parts, axis=0).astype(F16)
    parts = lax.all_to_all(parts, "y", 0, 0).astype(F32).sum(axis=0)
    part = [parts[i] * (1.0 / first[i]) for i in range(3)]
    away = swap(jnp.stack([(part[i] * second[i]).astype(F16) for i in range(3)]), "zh").astype(F32)
    gate_val, up_val, hidden_grad = [part[i] + away[i] * (1.0 / second[i]) for i in range(3)]

    sig_val = jax.nn.sigmoid(gate_val)
    hidden = gate_val * sig_val * up_val
    up_diff = hidden_grad * gate_val * sig_val
    gate_diff = hidden_grad * up_val * sig_val * (1.0 + gate_val * (1.0 - sig_val))
    mid = gather(jnp.stack([hidden.astype(BF16), gate_diff.astype(BF16), up_diff.astype(BF16)]), "y")

    body = functools.partial(partial_outs, n_x)
    flat = ((3, near * share, units), BF16)
    away, far_mid = call(body, (mid[near:],) + weights, (own.shape, BF16), flat)
    away = swap(away, "core")
    outs, near_mid = call(body, (mid[:near],) + weights, (own.shape, F32), flat)
    outs = (outs + away.astype(F32)).astype(BF16)
    outs = lax.all_to_all(outs, "x", 0, 0).astype(F32).sum(axis=0)
    outs = outs.astype(BF16).reshape(2, n_gx, rows, width).transpose(1, 0, 2, 3)
    outs = outs.reshape(n_gx, 2 * rows, width)
    outs, near_mid, far_mid, own, other = lax.optimization_barrier((outs, near_mid, far_mid, own, other))
    outs = lax.all_to_all(outs, "gx", 0, 0).astype(F32).sum(axis=0).astype(BF16)

    half = near * share
    hidden, gate_diff, up_diff = [jnp.concatenate([near_mid[i], far_mid[i]], axis=0) for i in range(3)]
    tok_rows, grad_rows = [
        jnp.concatenate([own[:, i].reshape(half, width), other[:, i].reshape(half, width)], axis=0)
        for i in range(2)
    ]
    down_grad = dot(hidden, grad_rows, 0, 0).astype(BF16)
    gate_grad = dot(gate_diff, tok_rows, 0, 0).astype(BF16)
    up_grad = dot(up_diff, tok_rows, 0, 0).astype(BF16)
    return (outs[:rows], outs[rows:], gate_grad.T, up_grad.T, down_grad)


def solution(mesh):
    fine = Mesh(mesh.devices.reshape(8, 4, 2, 2, 4), ("gx", "x", "core", "zh", "y"))
    hid, dim = ("gx", "x", "core"), ("zh", "y")
    act = P(hid, dim)
    return jax.shard_map(
        on_device,
        mesh=fine,
        in_specs=(act, P(dim, hid), P(dim, hid), act, act),
        out_specs=(act, act, P(dim, hid), P(dim, hid), act),
        check_vma=False,
    )
```

```python
import functools
import math

import jax
import jax.numpy as jnp
from jax import lax
from jax.experimental import pallas as pl
from jax.experimental.pallas import tpu as pltpu
from jax.sharding import Mesh, PartitionSpec as P

BF16 = jnp.bfloat16
F16 = jnp.float16
F32 = jnp.float32
VMEM = pl.BlockSpec(memory_space=pltpu.VMEM)
LIMIT = pltpu.CompilerParams(vmem_limit_bytes=40 * 1024 * 1024)


def dot(a, b, ca, cb):
    return lax.dot_general(a, b, (((ca,), (cb,)), ((), ())), preferred_element_type=F32)


def gather(part, axis):
    count = lax.axis_size(axis)
    return lax.all_to_all(jnp.broadcast_to(part[None], (count,) + part.shape), axis, 0, 0)


def swap(part, axis):
    return lax.ppermute(part, axis, [(0, 1), (1, 0)])


def scales(over):
    gate = 2.0 ** math.floor(math.log2(65504 / (over * 6 * 0.0625)))
    grad = 2.0 ** math.floor(math.log2(65504 / (over * 1.5 * 0.0390625)))
    return gate, gate, grad


def partial_sums(scale, rows_ref, gate_ref, up_ref, down_ref, *rest):
    done_ref, out_ref = rest if len(rest) == 2 else (None, rest[0])
    n_x, _, piece, width = rows_ref.shape
    n_y, halves, _, share, _ = out_ref.shape
    tok = rows_ref[:, 0].reshape(n_x * piece, width)
    grad = rows_ref[:, 1].reshape(n_x * piece, width)
    for which, (weight_ref, rows) in enumerate(((gate_ref, tok), (up_ref, tok), (down_ref, grad))):
        part = dot(weight_ref[...], rows, 1, 1) * scale[which]
        for y in range(n_y):
            out_ref[y, halves - 1, which] = part[y * share : (y + 1) * share]
            if done_ref is not None:
                out_ref[y, 0, which] = done_ref[y, 0, which]


def all_units(mid_ref, half, which):
    blocks = [mid_ref[y, half, which].astype(F32) for y in range(mid_ref.shape[0])]
    return jnp.concatenate(blocks, axis=0).astype(BF16)


def partial_outs(half, mid_ref, gate_ref, up_ref, down_ref, out_ref):
    n_x, _, _, width = out_ref.shape
    hidden, gate_diff, up_diff = [all_units(mid_ref, half, which) for which in range(3)]
    mixed = dot(hidden, down_ref[...], 0, 0)
    back = dot(gate_diff, gate_ref[...], 0, 0) + dot(up_diff, up_ref[...], 0, 0)
    out_ref[:, 0] = mixed.astype(out_ref.dtype).reshape(n_x, -1, width)
    out_ref[:, 1] = back.astype(out_ref.dtype).reshape(n_x, -1, width)


def outs_and_grads(mid_ref, own_ref, other_ref, gate_ref, up_ref, down_ref, out_ref, *rest):
    hbm, (grad_ref, sems) = rest[:3], rest[3:]
    width = down_ref.shape[1]
    copies = []
    for which in range(3):
        kind = 1 if which == 0 else 0
        rows = [ref[:, kind].reshape(-1, width) for ref in (own_ref, other_ref)]
        diff = jnp.concatenate([all_units(mid_ref, half, which) for half in range(2)], axis=1)
        grad_ref[which] = dot(diff, jnp.concatenate(rows, axis=0), 1, 0).astype(BF16)
        copies.append(pltpu.make_async_copy(grad_ref.at[which], hbm[which], sems.at[which]))
        copies[-1].start()
    partial_outs(0, mid_ref, gate_ref, up_ref, down_ref, out_ref)
    for copy in copies:
        copy.wait()


def call(body, inputs, *outs):
    return pl.pallas_call(
        body,
        out_shape=[jax.ShapeDtypeStruct(shape, dtype) for shape, dtype in outs],
        in_specs=[VMEM] * len(inputs),
        out_specs=[VMEM] * len(outs),
        compiler_params=LIMIT,
    )(*inputs)


def on_device(tokens, gate_weight, up_weight, down_weight, out_grad):
    rows, width = tokens.shape
    n_gx, n_x, n_y = lax.axis_size("gx"), lax.axis_size("x"), lax.axis_size("y")
    units = gate_weight.shape[1]
    weights = (gate_weight.T, up_weight.T, down_weight)
    both = jnp.concatenate([tokens, out_grad], axis=0)
    both = gather(both, "gx").reshape(n_gx, 2, rows, width).transpose(1, 0, 2, 3)
    own = gather(both.reshape(2, n_gx * rows, width), "x")
    other = swap(own, "core")

    first = scales(width)
    share = units // n_y
    sums = functools.partial(partial_sums, first)
    half = n_x * n_gx * rows
    parts = call(sums, (own,) + weights, ((n_y, 1, 3, share, half), F32))
    parts = call(sums, (other,) + weights + tuple(parts), ((n_y, 2, 3, share, half), F32))[0]
    parts = lax.all_to_all(parts.astype(F16), "y", 0, 0).astype(F32).sum(axis=0) * (1.0 / n_y)
    parts = parts + swap(parts.astype(F16), "zh").astype(F32)
    gate_val, up_val, hidden_grad = [parts[:, i] * (n_y / first[i]) for i in range(3)]

    sig_val = jax.nn.sigmoid(gate_val)
    hidden = gate_val * sig_val * up_val
    up_diff = hidden_grad * gate_val * sig_val
    gate_diff = hidden_grad * up_val * sig_val * (1.0 + gate_val * (1.0 - sig_val))
    mid = jnp.stack([hidden.astype(BF16), gate_diff.astype(BF16), up_diff.astype(BF16)], axis=1)
    mid = gather(mid, "y")

    away = call(functools.partial(partial_outs, 1), (mid,) + weights, (own.shape, BF16))[0]
    away = swap(away, "core")
    inputs = (mid, own, other) + weights
    grads = jax.ShapeDtypeStruct(down_weight.shape, BF16)
    outs, down_grad, gate_grad, up_grad = pl.pallas_call(
        outs_and_grads,
        out_shape=[jax.ShapeDtypeStruct(own.shape, F32)] + [grads] * 3,
        in_specs=[VMEM] * len(inputs),
        out_specs=[VMEM] + [pl.BlockSpec(memory_space=pl.ANY)] * 3,
        scratch_shapes=[pltpu.VMEM((3,) + down_weight.shape, BF16), pltpu.SemaphoreType.DMA((3,))],
        compiler_params=LIMIT,
    )(*inputs)
    outs = (outs + away.astype(F32)).astype(BF16)
    outs = lax.all_to_all(outs, "x", 0, 0).astype(F32).sum(axis=0)
    outs = outs.astype(BF16).reshape(2, n_gx, rows, width).transpose(1, 0, 2, 3)
    outs = outs.reshape(n_gx, 2 * rows, width)
    outs = lax.all_to_all(outs, "gx", 0, 0).astype(F32).sum(axis=0).astype(BF16)

    return (outs[:rows], outs[rows:], gate_grad.T, up_grad.T, down_grad)


def solution(mesh):
    fine = Mesh(mesh.devices.reshape(8, 4, 2, 2, 4), ("gx", "x", "core", "zh", "y"))
    hid, dim = ("gx", "x", "core"), ("zh", "y")
    act = P(hid, dim)
    return jax.shard_map(
        on_device,
        mesh=fine,
        in_specs=(act, P(dim, hid), P(dim, hid), act, act),
        out_specs=(act, act, P(dim, hid), P(dim, hid), act),
        check_vma=False,
    )
```

```python
import functools
import math

import jax
import jax.numpy as jnp
from jax import lax
from jax.experimental import pallas as pl
from jax.experimental.pallas import tpu as pltpu
from jax.sharding import Mesh, PartitionSpec as P

BF16 = jnp.bfloat16
F16 = jnp.float16
F32 = jnp.float32
VMEM = pl.BlockSpec(memory_space=pltpu.VMEM)
LIMIT = pltpu.CompilerParams(vmem_limit_bytes=20 * 1024 * 1024)


def dot(a, b, ca, cb):
    return lax.dot_general(a, b, (((ca,), (cb,)), ((), ())), preferred_element_type=F32)


def gather(part, axis):
    count = lax.axis_size(axis)
    return lax.all_to_all(jnp.broadcast_to(part[None], (count,) + part.shape), axis, 0, 0)


def swap(part, axis):
    return lax.ppermute(part, axis, [(0, 1), (1, 0)])


def scales(over):
    gate = 2.0 ** math.floor(math.log2(65504 / (over * 6 * 0.0625)))
    grad = 2.0 ** math.floor(math.log2(65504 / (over * 1.5 * 0.0390625)))
    return gate, gate, grad


def partial_sums(scale, rows_ref, mine_ref, peer_ref, out_ref):
    n_x, _, piece, width = rows_ref.shape
    n_y, _, _, share, _ = out_ref.shape
    tok = rows_ref[:, 0].reshape(n_x * piece, width)
    grad = rows_ref[:, 1].reshape(n_x * piece, width)
    for core, ref in enumerate((mine_ref, peer_ref)):
        for which, rows in enumerate((tok, tok, grad)):
            part = dot(ref[which], rows, 1, 1) * scale[which]
            for y in range(n_y):
                out_ref[y, core, which] = part[y * share : (y + 1) * share]


def all_units(mid_ref, *where):
    blocks = [mid_ref[(y,) + where].astype(F32) for y in range(mid_ref.shape[0])]
    return jnp.concatenate(blocks, axis=0).astype(BF16)


def partial_outs(mid_ref, own_ref, mine_ref, peer_ref, out_ref, give_ref):
    n_x, _, piece, width = out_ref.shape
    n_y, _, _, share, lanes = mid_ref.shape
    step = 2 * piece
    for block in range(width // lanes):
        rows = own_ref[:, :, :, block * lanes : (block + 1) * lanes]
        give_ref[:, block * step : (block + 1) * step] = rows.reshape(n_x, step, lanes)
    slot = (give_ref.shape[1] - step * (width // lanes)) // 3
    for which in range(3):
        at = step * (width // lanes) + which * slot
        for y in range(n_y):
            values = mid_ref[y, 1, which].astype(F32)
            values = jnp.concatenate([values, jnp.zeros((slot - share, lanes), F32)], axis=0)
            give_ref[y, at : at + slot] = values.astype(BF16)
    mixed, back = 0.0, 0.0
    for core, ref in enumerate((mine_ref, peer_ref)):
        hidden, gate_diff, up_diff = [all_units(mid_ref, core, which) for which in range(3)]
        mixed += dot(hidden, ref[2], 0, 0)
        back += dot(gate_diff, ref[0], 0, 0) + dot(up_diff, ref[1], 0, 0)
    out_ref[:, 0] = mixed.astype(out_ref.dtype).reshape(n_x, -1, width)
    out_ref[:, 1] = back.astype(out_ref.dtype).reshape(n_x, -1, width)


def weight_grads(mid_ref, got_ref, own_ref, down_hbm, gate_hbm, up_hbm, grad_ref, sems):
    n_x, _, piece, width = own_ref.shape
    n_y, _, _, share, lanes = mid_ref.shape
    step = 2 * piece
    base = step * (width // lanes)
    slot = (got_ref.shape[1] - base) // 3
    copies = []
    for which, hbm in enumerate((down_hbm, gate_hbm, up_hbm)):
        kind = 1 if which == 0 else 0
        far_rows = [
            got_ref[:, block * step + kind * piece : block * step + (kind + 1) * piece].reshape(n_x * piece, lanes)
            for block in range(width // lanes)
        ]
        rows = jnp.concatenate([own_ref[:, kind].reshape(-1, width), jnp.concatenate(far_rows, axis=1)], axis=0)
        at = base + which * slot
        far = [got_ref[y, at : at + slot].astype(F32)[:share] for y in range(n_y)]
        diff = jnp.concatenate([all_units(mid_ref, 0, which), jnp.concatenate(far, axis=0).astype(BF16)], axis=1)
        grad_ref[which] = dot(diff, rows, 1, 0).astype(BF16)
        copies.append(pltpu.make_async_copy(grad_ref.at[which], hbm, sems.at[which]))
        copies[-1].start()
    for copy in copies:
        copy.wait()


def call(body, inputs, *outs):
    return pl.pallas_call(
        body,
        out_shape=[jax.ShapeDtypeStruct(shape, dtype) for shape, dtype in outs],
        in_specs=[VMEM] * len(inputs),
        out_specs=[VMEM] * len(outs),
        compiler_params=LIMIT,
    )(*inputs)


def on_device(tokens, gate_weight, up_weight, down_weight, out_grad):
    rows, width = tokens.shape
    n_gx, n_x, n_y = lax.axis_size("gx"), lax.axis_size("x"), lax.axis_size("y")
    units = gate_weight.shape[1]
    mine = jnp.stack([gate_weight.T, up_weight.T, down_weight])
    peer = swap(mine, "core")

    both = jnp.concatenate([tokens, out_grad], axis=0)
    both = gather(both, "gx").reshape(n_gx, 2, rows, width).transpose(1, 0, 2, 3)
    own = gather(both.reshape(2, n_gx * rows, width), "x")

    first = scales(width)
    share = units // n_y
    half = n_x * n_gx * rows
    parts = call(functools.partial(partial_sums, first), (own, mine, peer), ((n_y, 2, 3, share, half), F32))[0]
    parts = lax.all_to_all(parts.astype(F16), "y", 0, 0).astype(F32).sum(axis=0) * (1.0 / n_y)
    away = parts.astype(F16)
    parts = parts + swap(away, "zh").astype(F32)
    gate_val, up_val, hidden_grad = [parts[:, i] * (n_y / first[i]) for i in range(3)]

    sig_val = jax.nn.sigmoid(gate_val)
    hidden = gate_val * sig_val * up_val
    up_diff = hidden_grad * gate_val * sig_val
    gate_diff = hidden_grad * up_val * sig_val * (1.0 + gate_val * (1.0 - sig_val))
    mid = jnp.stack([hidden.astype(BF16), gate_diff.astype(BF16), up_diff.astype(BF16)], axis=1)
    mid = gather(mid, "y")

    slot = -(-share // 16) * 16
    give = (n_x, own[0].size // half + 3 * slot, half)
    outs, give = call(partial_outs, (mid, own, mine, peer), (own.shape, BF16), (give, BF16))
    got = swap(give, "core")
    outs = lax.all_to_all(outs, "x", 0, 0).astype(F32).sum(axis=0)
    outs = outs.astype(BF16).reshape(2, n_gx, rows, width).transpose(1, 0, 2, 3)
    outs = outs.reshape(n_gx, 2 * rows, width)
    outs, got = lax.optimization_barrier((outs, got))
    outs = lax.all_to_all(outs, "gx", 0, 0).astype(F32).sum(axis=0).astype(BF16)

    grads = jax.ShapeDtypeStruct(down_weight.shape, BF16)
    down_grad, gate_grad, up_grad = pl.pallas_call(
        weight_grads,
        out_shape=[grads] * 3,
        in_specs=[VMEM] * 3,
        out_specs=[pl.BlockSpec(memory_space=pl.ANY)] * 3,
        scratch_shapes=[pltpu.VMEM((3,) + down_weight.shape, BF16), pltpu.SemaphoreType.DMA((3,))],
        compiler_params=LIMIT,
    )(mid, got, own)

    return (outs[:rows], outs[rows:], gate_grad.T, up_grad.T, down_grad)


def solution(mesh):
    fine = Mesh(mesh.devices.reshape(8, 4, 2, 2, 4), ("gx", "x", "core", "zh", "y"))
    hid, dim = ("gx", "x", "core"), ("zh", "y")
    act = P(hid, dim)
    return jax.shard_map(
        on_device,
        mesh=fine,
        in_specs=(act, P(dim, hid), P(dim, hid), act, act),
        out_specs=(act, act, P(dim, hid), P(dim, hid), act),
        check_vma=False,
    )
```

```python
import functools
import math

import jax
import jax.numpy as jnp
from jax import lax
from jax.experimental import pallas as pl
from jax.experimental.pallas import tpu as pltpu
from jax.sharding import Mesh, PartitionSpec as P

BF16 = jnp.bfloat16
F16 = jnp.float16
F32 = jnp.float32
VMEM = pl.BlockSpec(memory_space=pltpu.VMEM)
LIMIT = pltpu.CompilerParams(vmem_limit_bytes=20 * 1024 * 1024)


def dot(a, b, ca, cb):
    return lax.dot_general(a, b, (((ca,), (cb,)), ((), ())), preferred_element_type=F32)


def gather(part, axis):
    count = lax.axis_size(axis)
    return lax.all_to_all(jnp.broadcast_to(part[None], (count,) + part.shape), axis, 0, 0)


def swap(part, axis):
    return lax.ppermute(part, axis, [(0, 1), (1, 0)])


def scales(over):
    gate = 2.0 ** math.floor(math.log2(65504 / (over * 6 * 0.0625)))
    grad = 2.0 ** math.floor(math.log2(65504 / (over * 1.5 * 0.0390625)))
    return gate, gate, grad


def partial_sums(scale, rows_ref, mine_ref, peer_ref, out_ref):
    n_x, _, piece, width = rows_ref.shape
    n_y, _, _, share, _ = out_ref.shape
    tok = rows_ref[:, 0].reshape(n_x * piece, width)
    grad = rows_ref[:, 1].reshape(n_x * piece, width)
    for core, ref in enumerate((mine_ref, peer_ref)):
        for which, rows in enumerate((tok, tok, grad)):
            part = dot(ref[which], rows, 1, 1) * scale[which]
            for y in range(n_y):
                out_ref[y, core, which] = part[y * share : (y + 1) * share]


def all_units(mid_ref, *where):
    blocks = [mid_ref[(y,) + where].astype(F32) for y in range(mid_ref.shape[0])]
    return jnp.concatenate(blocks, axis=0).astype(BF16)


def partial_outs(mid_ref, own_ref, mine_ref, peer_ref, out_ref, give_ref):
    n_x, _, piece, width = out_ref.shape
    n_y, _, _, share, lanes = mid_ref.shape
    step = 2 * piece
    for block in range(width // lanes):
        rows = own_ref[:, :, :, block * lanes : (block + 1) * lanes]
        give_ref[:, block * step : (block + 1) * step] = rows.reshape(n_x, step, lanes)
    slot = (give_ref.shape[1] - step * (width // lanes)) // 3
    for which in range(3):
        at = step * (width // lanes) + which * slot
        for y in range(n_y):
            values = mid_ref[y, 1, which].astype(F32)
            values = jnp.concatenate([values, jnp.zeros((slot - share, lanes), F32)], axis=0)
            give_ref[y, at : at + slot] = values.astype(BF16)
    mixed, back = 0.0, 0.0
    for core, ref in enumerate((mine_ref, peer_ref)):
        hidden, gate_diff, up_diff = [all_units(mid_ref, core, which) for which in range(3)]
        mixed += dot(hidden, ref[2], 0, 0)
        back += dot(gate_diff, ref[0], 0, 0) + dot(up_diff, ref[1], 0, 0)
    out_ref[:, 0] = mixed.astype(out_ref.dtype).reshape(n_x, -1, width)
    out_ref[:, 1] = back.astype(out_ref.dtype).reshape(n_x, -1, width)


def weight_grads(mid_ref, got_ref, own_ref, down_hbm, gate_hbm, up_hbm, grad_ref, sems):
    n_x, _, piece, width = own_ref.shape
    n_y, _, _, share, lanes = mid_ref.shape
    step = 2 * piece
    base = step * (width // lanes)
    slot = (got_ref.shape[1] - base) // 3
    copies = []
    for which, hbm in enumerate((down_hbm, gate_hbm, up_hbm)):
        kind = 1 if which == 0 else 0
        far_rows = [
            got_ref[:, block * step + kind * piece : block * step + (kind + 1) * piece].reshape(n_x * piece, lanes)
            for block in range(width // lanes)
        ]
        rows = jnp.concatenate([own_ref[:, kind].reshape(-1, width), jnp.concatenate(far_rows, axis=1)], axis=0)
        at = base + which * slot
        far = [got_ref[y, at : at + slot].astype(F32)[:share] for y in range(n_y)]
        diff = jnp.concatenate([all_units(mid_ref, 0, which), jnp.concatenate(far, axis=0).astype(BF16)], axis=1)
        grad_ref[which] = dot(diff, rows, 1, 0).astype(BF16)
        copies.append(pltpu.make_async_copy(grad_ref.at[which], hbm, sems.at[which]))
        copies[-1].start()
    for copy in copies:
        copy.wait()


def call(body, inputs, *outs):
    return pl.pallas_call(
        body,
        out_shape=[jax.ShapeDtypeStruct(shape, dtype) for shape, dtype in outs],
        in_specs=[VMEM] * len(inputs),
        out_specs=[VMEM] * len(outs),
        compiler_params=LIMIT,
    )(*inputs)


def on_device(tokens, gate_weight, up_weight, down_weight, out_grad):
    rows, width = tokens.shape
    n_gx, n_x, n_y = lax.axis_size("gx"), lax.axis_size("x"), lax.axis_size("y")
    units = gate_weight.shape[1]
    mine = jnp.stack([gate_weight.T, up_weight.T, down_weight])
    peer = swap(mine, "core")

    both = jnp.concatenate([tokens, out_grad], axis=0)
    both = gather(both, "gx").reshape(n_gx, 2, rows, width).transpose(1, 0, 2, 3)
    own = gather(both.reshape(2, n_gx * rows, width), "x")

    first = scales(width)
    share = units // n_y
    half = n_x * n_gx * rows
    parts = call(functools.partial(partial_sums, first), (own, mine, peer), ((n_y, 2, 3, share, half), F32))[0]
    parts = lax.all_to_all(parts.astype(F16), "y", 0, 0).astype(F32).sum(axis=0) * (1.0 / n_y)
    away = parts.astype(F16)
    parts = parts + swap(away, "zh").astype(F32)
    gate_val, up_val, hidden_grad = [parts[:, i] * (n_y / first[i]) for i in range(3)]

    sig_val = jax.nn.sigmoid(gate_val)
    hidden = gate_val * sig_val * up_val
    up_diff = hidden_grad * gate_val * sig_val
    gate_diff = hidden_grad * up_val * sig_val * (1.0 + gate_val * (1.0 - sig_val))
    mid = jnp.stack([hidden.astype(BF16), gate_diff.astype(BF16), up_diff.astype(BF16)], axis=1)
    mid = gather(mid, "y")

    slot = -(-share // 16) * 16
    give = (n_x, own[0].size // half + 3 * slot, half)
    outs, give = call(partial_outs, (mid, own, mine, peer), (own.shape, BF16), (give, BF16))
    outs = lax.all_to_all(outs, "x", 0, 0).astype(F32).sum(axis=0)
    outs = outs.astype(BF16).reshape(2, n_gx, rows, width).transpose(1, 0, 2, 3)
    outs = outs.reshape(n_gx, 2 * rows, width)
    outs, give = lax.optimization_barrier((outs, give))
    got = swap(give, "core")
    outs = lax.all_to_all(outs, "gx", 0, 0)

    grads = jax.ShapeDtypeStruct(down_weight.shape, BF16)
    down_grad, gate_grad, up_grad = pl.pallas_call(
        weight_grads,
        out_shape=[grads] * 3,
        in_specs=[VMEM] * 3,
        out_specs=[pl.BlockSpec(memory_space=pl.ANY)] * 3,
        scratch_shapes=[pltpu.VMEM((3,) + down_weight.shape, BF16), pltpu.SemaphoreType.DMA((3,))],
        compiler_params=LIMIT,
    )(mid, got, own)

    outs, down_grad, gate_grad, up_grad = lax.optimization_barrier((outs, down_grad, gate_grad, up_grad))
    outs = outs.astype(F32).sum(axis=0).astype(BF16)
    return (outs[:rows], outs[rows:], gate_grad.T, up_grad.T, down_grad)


def solution(mesh):
    fine = Mesh(mesh.devices.reshape(8, 4, 2, 2, 4), ("gx", "x", "core", "zh", "y"))
    hid, dim = ("gx", "x", "core"), ("zh", "y")
    act = P(hid, dim)
    return jax.shard_map(
        on_device,
        mesh=fine,
        in_specs=(act, P(dim, hid), P(dim, hid), act, act),
        out_specs=(act, act, P(dim, hid), P(dim, hid), act),
        check_vma=False,
    )
```

```python
import functools
import math

import jax
import jax.numpy as jnp
from jax import lax
from jax.experimental import pallas as pl
from jax.experimental.pallas import tpu as pltpu
from jax.sharding import Mesh, PartitionSpec as P

BF16 = jnp.bfloat16
F16 = jnp.float16
F32 = jnp.float32
VMEM = pl.BlockSpec(memory_space=pltpu.VMEM)
LIMIT = pltpu.CompilerParams(vmem_limit_bytes=20 * 1024 * 1024)


def dot(a, b, ca, cb):
    return lax.dot_general(a, b, (((ca,), (cb,)), ((), ())), preferred_element_type=F32)


def gather(part, axis):
    count = lax.axis_size(axis)
    return lax.all_to_all(jnp.broadcast_to(part[None], (count,) + part.shape), axis, 0, 0)


def swap(part, axis):
    return lax.ppermute(part, axis, [(0, 1), (1, 0)])


def scales(over):
    gate = 2.0 ** math.floor(math.log2(65504 / (over * 6 * 0.0625)))
    grad = 2.0 ** math.floor(math.log2(65504 / (over * 1.5 * 0.0390625)))
    return gate, gate, grad


def partial_sums(scale, rows_ref, mine_ref, peer_ref, out_ref):
    n_x, _, piece, width = rows_ref.shape
    n_y, _, _, share, _ = out_ref.shape
    tok = rows_ref[:, 0].reshape(n_x * piece, width)
    grad = rows_ref[:, 1].reshape(n_x * piece, width)
    for core, ref in enumerate((mine_ref, peer_ref)):
        for which, rows in enumerate((tok, tok, grad)):
            part = dot(ref[which], rows, 1, 1) * scale[which]
            for y in range(n_y):
                out_ref[y, core, which] = part[y * share : (y + 1) * share]


def all_units(mid_ref, *where):
    blocks = [mid_ref[(y,) + where].astype(F32) for y in range(mid_ref.shape[0])]
    return jnp.concatenate(blocks, axis=0).astype(BF16)


def partial_outs(mid_ref, own_ref, mine_ref, peer_ref, out_ref, give_ref):
    n_x, _, piece, width = out_ref.shape
    n_y, _, _, share, lanes = mid_ref.shape
    step = 2 * piece
    for block in range(width // lanes):
        rows = own_ref[:, :, :, block * lanes : (block + 1) * lanes]
        give_ref[:, block * step : (block + 1) * step] = rows.reshape(n_x, step, lanes)
    slot = (give_ref.shape[1] - step * (width // lanes)) // 3
    for which in range(3):
        at = step * (width // lanes) + which * slot
        for y in range(n_y):
            values = mid_ref[y, 1, which].astype(F32)
            values = jnp.concatenate([values, jnp.zeros((slot - share, lanes), F32)], axis=0)
            give_ref[y, at : at + slot] = values.astype(BF16)
    mixed, back = 0.0, 0.0
    for core, ref in enumerate((mine_ref, peer_ref)):
        hidden, gate_diff, up_diff = [all_units(mid_ref, core, which) for which in range(3)]
        mixed += dot(hidden, ref[2], 0, 0)
        back += dot(gate_diff, ref[0], 0, 0) + dot(up_diff, ref[1], 0, 0)
    out_ref[:, 0] = mixed.astype(out_ref.dtype).reshape(n_x, -1, width)
    out_ref[:, 1] = back.astype(out_ref.dtype).reshape(n_x, -1, width)


def weight_grads(mid_ref, got_ref, own_ref, down_hbm, gate_hbm, up_hbm, grad_ref, sems):
    n_x, _, piece, width = own_ref.shape
    n_y, _, _, share, lanes = mid_ref.shape
    step = 2 * piece
    base = step * (width // lanes)
    slot = (got_ref.shape[1] - base) // 3
    copies = []
    for which, hbm in enumerate((down_hbm, gate_hbm, up_hbm)):
        kind = 1 if which == 0 else 0
        far_rows = [
            got_ref[:, block * step + kind * piece : block * step + (kind + 1) * piece].reshape(n_x * piece, lanes)
            for block in range(width // lanes)
        ]
        rows = jnp.concatenate([own_ref[:, kind].reshape(-1, width), jnp.concatenate(far_rows, axis=1)], axis=0)
        at = base + which * slot
        far = [got_ref[y, at : at + slot].astype(F32)[:share] for y in range(n_y)]
        diff = jnp.concatenate([all_units(mid_ref, 0, which), jnp.concatenate(far, axis=0).astype(BF16)], axis=1)
        grad_ref[which] = dot(diff, rows, 1, 0).astype(BF16)
        copies.append(pltpu.make_async_copy(grad_ref.at[which], hbm, sems.at[which]))
        copies[-1].start()
    for copy in copies:
        copy.wait()


def call(body, inputs, *outs):
    return pl.pallas_call(
        body,
        out_shape=[jax.ShapeDtypeStruct(shape, dtype) for shape, dtype in outs],
        in_specs=[VMEM] * len(inputs),
        out_specs=[VMEM] * len(outs),
        compiler_params=LIMIT,
    )(*inputs)


def on_device(tokens, gate_weight, up_weight, down_weight, out_grad):
    rows, width = tokens.shape
    n_gx, n_x, n_y = lax.axis_size("gx"), lax.axis_size("x"), lax.axis_size("y")
    units = gate_weight.shape[1]
    mine = jnp.zeros((3,) + down_weight.shape, BF16)
    for i, weight in enumerate((gate_weight.T, up_weight.T, down_weight)):
        mine = lax.dynamic_update_index_in_dim(mine, weight, lax.optimization_barrier(jnp.int32(i)), 0)
    peer = swap(mine, "core")

    both = jnp.concatenate([tokens, out_grad], axis=0)
    both = gather(both, "gx").reshape(n_gx, 2, rows, width).transpose(1, 0, 2, 3)
    own = gather(both.reshape(2, n_gx * rows, width), "x")

    first = scales(width)
    share = units // n_y
    half = n_x * n_gx * rows
    parts = call(functools.partial(partial_sums, first), (own, mine, peer), ((n_y, 2, 3, share, half), F32))[0]
    parts = lax.all_to_all(parts.astype(F16), "y", 0, 0).astype(F32).sum(axis=0) * (1.0 / n_y)
    away = parts.astype(F16)
    parts = parts + swap(away, "zh").astype(F32)
    gate_val, up_val, hidden_grad = [parts[:, i] * (n_y / first[i]) for i in range(3)]

    sig_val = jax.nn.sigmoid(gate_val)
    hidden = gate_val * sig_val * up_val
    up_diff = hidden_grad * gate_val * sig_val
    gate_diff = hidden_grad * up_val * sig_val * (1.0 + gate_val * (1.0 - sig_val))
    mid = jnp.stack([hidden.astype(BF16), gate_diff.astype(BF16), up_diff.astype(BF16)], axis=1)
    mid = gather(mid, "y")

    slot = -(-share // 16) * 16
    give = (n_x, own[0].size // half + 3 * slot, half)
    outs, give = call(partial_outs, (mid, own, mine, peer), (own.shape, BF16), (give, BF16))
    outs = lax.all_to_all(outs, "x", 0, 0).astype(F32).sum(axis=0)
    outs = outs.astype(BF16).reshape(2, n_gx, rows, width).transpose(1, 0, 2, 3)
    outs = outs.reshape(n_gx, 2 * rows, width)
    outs, give = lax.optimization_barrier((outs, give))
    got = swap(give, "core")
    outs = lax.all_to_all(outs, "gx", 0, 0)

    grads = jax.ShapeDtypeStruct(down_weight.shape, BF16)
    down_grad, gate_grad, up_grad = pl.pallas_call(
        weight_grads,
        out_shape=[grads] * 3,
        in_specs=[VMEM] * 3,
        out_specs=[pl.BlockSpec(memory_space=pl.ANY)] * 3,
        scratch_shapes=[pltpu.VMEM((3,) + down_weight.shape, BF16), pltpu.SemaphoreType.DMA((3,))],
        compiler_params=LIMIT,
    )(mid, got, own)

    outs, down_grad, gate_grad, up_grad = lax.optimization_barrier((outs, down_grad, gate_grad, up_grad))
    outs = outs.astype(F32).sum(axis=0).astype(BF16)
    return (outs[:rows], outs[rows:], gate_grad.T, up_grad.T, down_grad)


def solution(mesh):
    fine = Mesh(mesh.devices.reshape(8, 4, 2, 2, 4), ("gx", "x", "core", "zh", "y"))
    hid, dim = ("gx", "x", "core"), ("zh", "y")
    act = P(hid, dim)
    return jax.shard_map(
        on_device,
        mesh=fine,
        in_specs=(act, P(dim, hid), P(dim, hid), act, act),
        out_specs=(act, act, P(dim, hid), P(dim, hid), act),
        check_vma=False,
    )
```

```python
import functools
import math

import jax
import jax.numpy as jnp
from jax import lax
from jax.experimental import pallas as pl
from jax.experimental.pallas import tpu as pltpu
from jax.sharding import Mesh, PartitionSpec as P

BF16 = jnp.bfloat16
F16 = jnp.float16
F32 = jnp.float32
VMEM = pl.BlockSpec(memory_space=pltpu.VMEM)
LIMIT = pltpu.CompilerParams(vmem_limit_bytes=20 * 1024 * 1024)


def dot(a, b, ca, cb):
    return lax.dot_general(a, b, (((ca,), (cb,)), ((), ())), preferred_element_type=F32)


def gather(part, axis):
    count = lax.axis_size(axis)
    return lax.all_to_all(jnp.broadcast_to(part[None], (count,) + part.shape), axis, 0, 0)


def swap(part, axis):
    return lax.ppermute(part, axis, [(0, 1), (1, 0)])


def scales(over):
    gate = 2.0 ** math.floor(math.log2(65504 / (over * 6 * 0.0625)))
    grad = 2.0 ** math.floor(math.log2(65504 / (over * 1.5 * 0.0390625)))
    return gate, gate, grad


def partial_sums(scale, rows_ref, mine_ref, peer_ref, out_ref):
    n_x, _, piece, width = rows_ref.shape
    n_y, _, _, share, _ = out_ref.shape
    tok = rows_ref[:, 0].reshape(n_x * piece, width)
    grad = rows_ref[:, 1].reshape(n_x * piece, width)
    for core, ref in enumerate((mine_ref, peer_ref)):
        for which, rows in enumerate((tok, tok, grad)):
            part = dot(ref[which], rows, 1, 1) * scale[which]
            for y in range(n_y):
                out_ref[y, core, which] = part[y * share : (y + 1) * share]


def all_units(mid_ref, *where):
    blocks = [mid_ref[(y,) + where].astype(F32) for y in range(mid_ref.shape[0])]
    return jnp.concatenate(blocks, axis=0).astype(BF16)


def partial_outs(mid_ref, own_ref, mine_ref, peer_ref, out_ref, give_ref):
    n_x, _, piece, width = out_ref.shape
    n_y, _, _, share, lanes = mid_ref.shape
    step = 2 * piece
    for block in range(width // lanes):
        rows = own_ref[:, :, :, block * lanes : (block + 1) * lanes]
        give_ref[:, block * step : (block + 1) * step] = rows.reshape(n_x, step, lanes)
    slot = (give_ref.shape[1] - step * (width // lanes)) // 3
    for which in range(3):
        at = step * (width // lanes) + which * slot
        for y in range(n_y):
            values = mid_ref[y, 1, which].astype(F32)
            values = jnp.concatenate([values, jnp.zeros((slot - share, lanes), F32)], axis=0)
            give_ref[y, at : at + slot] = values.astype(BF16)
    mixed, back = 0.0, 0.0
    for core, ref in enumerate((mine_ref, peer_ref)):
        hidden, gate_diff, up_diff = [all_units(mid_ref, core, which) for which in range(3)]
        mixed += dot(hidden, ref[2], 0, 0)
        back += dot(gate_diff, ref[0], 0, 0) + dot(up_diff, ref[1], 0, 0)
    out_ref[:, 0] = mixed.astype(out_ref.dtype).reshape(n_x, -1, width)
    out_ref[:, 1] = back.astype(out_ref.dtype).reshape(n_x, -1, width)


def weight_grads(mid_ref, got_ref, own_ref, down_hbm, gate_hbm, up_hbm, grad_ref, sems):
    n_x, _, piece, width = own_ref.shape
    n_y, _, _, share, lanes = mid_ref.shape
    step = 2 * piece
    base = step * (width // lanes)
    slot = (got_ref.shape[1] - base) // 3
    copies = []
    for which, hbm in enumerate((down_hbm, gate_hbm, up_hbm)):
        kind = 1 if which == 0 else 0
        far_rows = [
            got_ref[:, block * step + kind * piece : block * step + (kind + 1) * piece].reshape(n_x * piece, lanes)
            for block in range(width // lanes)
        ]
        rows = jnp.concatenate([own_ref[:, kind].reshape(-1, width), jnp.concatenate(far_rows, axis=1)], axis=0)
        at = base + which * slot
        far = [got_ref[y, at : at + slot].astype(F32)[:share] for y in range(n_y)]
        diff = jnp.concatenate([all_units(mid_ref, 0, which), jnp.concatenate(far, axis=0).astype(BF16)], axis=1)
        grad_ref[which] = dot(diff, rows, 1, 0).astype(BF16)
        copies.append(pltpu.make_async_copy(grad_ref.at[which], hbm, sems.at[which]))
        copies[-1].start()
    for copy in copies:
        copy.wait()


def call(body, inputs, *outs):
    return pl.pallas_call(
        body,
        out_shape=[jax.ShapeDtypeStruct(shape, dtype) for shape, dtype in outs],
        in_specs=[VMEM] * len(inputs),
        out_specs=[VMEM] * len(outs),
        compiler_params=LIMIT,
    )(*inputs)


def on_device(tokens, gate_weight, up_weight, down_weight, out_grad):
    rows, width = tokens.shape
    n_gx, n_x, n_y = lax.axis_size("gx"), lax.axis_size("x"), lax.axis_size("y")
    units = gate_weight.shape[1]
    mine = jnp.broadcast_to(down_weight[None], (3,) + down_weight.shape)
    for i, weight in enumerate((gate_weight.T, up_weight.T)):
        mine = lax.dynamic_update_index_in_dim(mine, weight, lax.optimization_barrier(jnp.int32(i)), 0)
    peer = swap(mine, "core")

    both = jnp.concatenate([tokens, out_grad], axis=0)
    both = gather(both, "gx").reshape(n_gx, 2, rows, width).transpose(1, 0, 2, 3)
    own = gather(both.reshape(2, n_gx * rows, width), "x")

    first = scales(width)
    share = units // n_y
    half = n_x * n_gx * rows
    parts = call(functools.partial(partial_sums, first), (own, mine, peer), ((n_y, 2, 3, share, half), F32))[0]
    parts = lax.all_to_all(parts.astype(F16), "y", 0, 0).astype(F32).sum(axis=0) * (1.0 / n_y)
    away = parts.astype(F16)
    parts = parts + swap(away, "zh").astype(F32)
    gate_val, up_val, hidden_grad = [parts[:, i] * (n_y / first[i]) for i in range(3)]

    sig_val = jax.nn.sigmoid(gate_val)
    hidden = gate_val * sig_val * up_val
    up_diff = hidden_grad * gate_val * sig_val
    gate_diff = hidden_grad * up_val * sig_val * (1.0 + gate_val * (1.0 - sig_val))
    mid = jnp.stack([hidden.astype(BF16), gate_diff.astype(BF16), up_diff.astype(BF16)], axis=1)
    mid = gather(mid, "y")

    slot = -(-share // 16) * 16
    give = (n_x, own[0].size // half + 3 * slot, half)
    outs, give = call(partial_outs, (mid, own, mine, peer), (own.shape, BF16), (give, BF16))
    outs = lax.all_to_all(outs, "x", 0, 0).astype(F32).sum(axis=0)
    outs = outs.astype(BF16).reshape(2, n_gx, rows, width).transpose(1, 0, 2, 3)
    outs = outs.reshape(n_gx, 2 * rows, width)
    outs, give = lax.optimization_barrier((outs, give))
    got = swap(give, "core")
    outs = lax.all_to_all(outs, "gx", 0, 0)

    grads = jax.ShapeDtypeStruct(down_weight.shape, BF16)
    down_grad, gate_grad, up_grad = pl.pallas_call(
        weight_grads,
        out_shape=[grads] * 3,
        in_specs=[VMEM] * 3,
        out_specs=[pl.BlockSpec(memory_space=pl.ANY)] * 3,
        scratch_shapes=[pltpu.VMEM((3,) + down_weight.shape, BF16), pltpu.SemaphoreType.DMA((3,))],
        compiler_params=LIMIT,
    )(mid, got, own)

    outs, down_grad, gate_grad, up_grad = lax.optimization_barrier((outs, down_grad, gate_grad, up_grad))
    outs = outs.astype(F32).sum(axis=0).astype(BF16)
    return (outs[:rows], outs[rows:], gate_grad.T, up_grad.T, down_grad)


def solution(mesh):
    fine = Mesh(mesh.devices.reshape(8, 4, 2, 2, 4), ("gx", "x", "core", "zh", "y"))
    hid, dim = ("gx", "x", "core"), ("zh", "y")
    act = P(hid, dim)
    return jax.shard_map(
        on_device,
        mesh=fine,
        in_specs=(act, P(dim, hid), P(dim, hid), act, act),
        out_specs=(act, act, P(dim, hid), P(dim, hid), act),
        check_vma=False,
    )
```
